512 devices in a mesh: dp: 64 (over z, x), crop: 2 (over core), proto: 4 (over y).
Axes of the slice: x: 4, y: 4, z: 16, core: 2. Of those that a mesh axis runs over, the one named last changes fastest.
Arguments:
- features: bfloat16 [2, 3072, 256], P('crop', 'dp'), may hold values from -6 to 6
- targets: bfloat16 [3072, 131072], P('crop', ('dp', 'proto')), may hold values from 9.968062e-10 to 9.9658966e-05
- partner: int32 [2, 192], P('crop'), may hold values from 0 to 191
- vectors: float32 [131072, 256], P(('dp', 'proto', 'crop')), may hold values from -0.375 to 0.375
- first: float32 [131072, 256], P(('dp', 'proto', 'crop')), may hold values from -0.0014648438 to 0.0014648438
- second: float32 [131072, 256], P(('dp', 'proto', 'crop')), may hold values from 1e-08 to 1e-07
- teacher: float32 [131072, 256], P(('dp', 'proto', 'crop')), may hold values from -0.375 to 0.375
Outputs:
- grad_features: float32 [2, 3072, 256], P('crop', 'dp')
- new_vectors: float32 [131072, 256], P(('dp', 'proto', 'crop'))
- new_first: float32 [131072, 256], P(('dp', 'proto', 'crop'))
- new_second: float32 [131072, 256], P(('dp', 'proto', 'crop'))
- new_teacher: float32 [131072, 256], P(('dp', 'proto', 'crop'))
The draws below stay inside these ranges and needn't reach their ends.
All inputs are finite; a program needn't handle non-finite values.
Results may differ from the reference program's by a relative error of at most 0.004.
The reference program's roundings to bfloat16 on the way count: a program that leaves them out, or rounds other values in their place, can miss the bound.
Values may be sent and summed in bfloat16 or wider, within the bound.
No kernel may reach another device: no remote copies, remote signals or barrier semaphores. Data moves between devices by JAX's collectives and lax.ppermute only.
A program may use at most 64 MiB of HBM per device.

```python
import math
import jax
import jax.numpy as jnp
from jax import lax

EMBED = 256
PROTOS = 131072
TILE = 16
GROUP = 3072


def with_ends(array, rng, low, largest):
    shape = array.shape
    place = [jax.random.randint(jax.random.fold_in(rng, axis), (), 0, shape[axis]) for axis in range(len(shape))]
    array = array.at[tuple(place)].set(low)
    longest = shape.index(max(shape))
    place[longest] = (place[longest] + 1) % shape[longest]
    return array.at[tuple(place)].set(largest)


def steps_of(stream_key, shape, pieces, smallest, largest):
    gain = 1.0
    for axis_at, blocks in pieces:
        draws = jax.random.uniform(jax.random.fold_in(jax.random.fold_in(stream_key, 6), axis_at), (blocks,), jnp.float32, smallest / len(pieces), largest / len(pieces))
        gain = gain * jnp.repeat(jnp.exp(draws), shape[axis_at] // blocks).reshape((-1,) + (1,) * (len(shape) - 1 - axis_at))
    return gain


def gaussian(own_key, shape, deviation, most, cuts=(), kind=jnp.bfloat16):
    entries = deviation * jax.random.normal(own_key, shape, jnp.float32)
    if cuts:
        entries = entries * steps_of(own_key, shape, cuts, -0.22, 0.18)
    return jnp.clip(entries, -most, most).astype(kind)


def setup_inputs(seed: int = 0) -> dict:
    seeds = jax.random.split(jax.random.key(seed), 8)
    features = gaussian(seeds[0], (2, GROUP, EMBED), 1.0, 6.0, ((0, 2), (1, 64)))
    targets = jnp.clip(jnp.exp(math.log(9.965896606445312e-05) - 11.5127082 * jax.random.uniform(seeds[1], (GROUP, PROTOS), jnp.float32) ** steps_of(seeds[1], (GROUP, PROTOS), ((0, 2), (1, 256)), -0.2, 0.2)), 9.968061931431293e-10, 9.965896606445312e-05).astype(jnp.bfloat16)
    partner = with_ends(jax.random.randint(seeds[2], (2, GROUP // TILE), 0, GROUP // TILE), jax.random.fold_in(seeds[2], 1), 0, (GROUP // TILE) - 1).astype(jnp.int32)
    vectors = gaussian(seeds[3], (PROTOS, EMBED), EMBED ** -0.5, 0.375, ((0, 512),), jnp.float32)
    first = gaussian(seeds[4], (PROTOS, EMBED), 0.0001, 0.0014648438, ((0, 512),), jnp.float32)
    second = jnp.clip(jnp.exp(math.log(1.0000000116860974e-07) - 2.3025851 * jax.random.uniform(seeds[5], (PROTOS, EMBED), jnp.float32) ** steps_of(seeds[5], (PROTOS, EMBED), ((0, 512),), -0.2, 0.2)), 9.99999993922529e-09, 1.0000000116860974e-07)
    teacher = gaussian(seeds[6], (PROTOS, EMBED), EMBED ** -0.5, 0.375, ((0, 512),), jnp.float32)
    return {"features": features, "targets": targets, "partner": partner, "vectors": vectors, "first": first, "second": second, "teacher": teacher}


student_temp = 0.1
norm_eps = 1e-06
learn_rate = 0.01
weight_decay = 0.04
beta_first = 0.9
beta_second = 0.999
bias_first = 0.9999734386011124
bias_second = 0.0952078536
adam_eps = 1e-08
teacher_keep = 0.996

def norm_back(upstream, feats):
    length = jnp.sqrt(lax.optimization_barrier(jnp.sum(feats * feats, 1, keepdims=True)) + norm_eps)
    unit = feats / length
    return (upstream - unit * lax.optimization_barrier(jnp.sum(unit * upstream, 1, keepdims=True))) / length

def adamw_rows(grad_rows, vectors, first, second, teacher):
    vlen = jnp.sqrt(lax.optimization_barrier(jnp.sum(vectors * vectors, 1, keepdims=True)) + norm_eps)
    unit = vectors / vlen
    dvec = (grad_rows - unit * lax.optimization_barrier(jnp.sum(unit * grad_rows, 1, keepdims=True))) / vlen
    new_first = beta_first * first + (1.0 - beta_first) * dvec
    new_second = beta_second * second + (1.0 - beta_second) * dvec * dvec
    update = new_first / bias_first / (jnp.sqrt(new_second / bias_second) + adam_eps) + weight_decay * vectors
    new_vectors = vectors - learn_rate * update
    new_teacher = teacher_keep * teacher + (1.0 - teacher_keep) * new_vectors
    return (new_vectors, new_first, new_second, new_teacher)

def reference(features, targets, partner, vectors, first, second, teacher):
    vlen = jnp.sqrt(lax.optimization_barrier(jnp.sum(vectors * vectors, 1, keepdims=True)) + norm_eps)
    direction = (vectors / vlen).astype(jnp.bfloat16)
    block = min(PROTOS, 4096)
    nblocks = PROTOS // block
    wblocks = direction.reshape(nblocks, block, EMBED)
    indices = jnp.arange(nblocks, dtype=jnp.int32)
    ddir = jnp.zeros((PROTOS, EMBED), jnp.float32)
    grads = []
    for group in range(2):
        feats = features[group].astype(jnp.float32)
        length = jnp.sqrt(lax.optimization_barrier(jnp.sum(feats * feats, 1, keepdims=True)) + norm_eps)
        unit = (feats / length).astype(jnp.bfloat16)
        rows = (partner[group][:, None] * TILE + jnp.arange(TILE, dtype=jnp.int32)[None, :]).reshape(-1).astype(jnp.int32)

        def block_terms(index):
            wblk = wblocks[index]
            start = (index * block).astype(jnp.int32)
            tblk = lax.dynamic_slice_in_dim(targets, start, block, 1)[rows].astype(jnp.float32)
            scores = lax.dot_general(unit, wblk, (((1,), (1,)), ((), ())), preferred_element_type=jnp.float32)
            expo = jnp.exp(scores / student_temp - 1.0 / student_temp)
            return (wblk, tblk, expo)

        def totals(carry, index):
            wblk, tblk, expo = block_terms(index)
            return ((carry[0] + lax.optimization_barrier(jnp.sum(expo, 1)), carry[1] + lax.optimization_barrier(jnp.sum(tblk, 1))), None)
        zero_rows = jnp.zeros((GROUP,), jnp.float32)
        (exp_total, target_total), unused = lax.scan(totals, (zero_rows, zero_rows), indices)

        def backward(carry, index):
            wblk, tblk, expo = block_terms(index)
            dscore = ((expo / exp_total[:, None] * target_total[:, None] - tblk) / student_temp).astype(jnp.bfloat16)
            carry = carry + jnp.dot(dscore, wblk, preferred_element_type=jnp.float32)
            dblk = lax.dot_general(dscore, unit, (((0,), (0,)), ((), ())), preferred_element_type=jnp.float32)
            return (carry, dblk)
        dunit, dblocks = lax.scan(backward, jnp.zeros((GROUP, EMBED), jnp.float32), indices)
        ddir = ddir + dblocks.reshape(PROTOS, EMBED)
        grads.append(norm_back(dunit, feats))
    new_vectors, new_first, new_second, new_teacher = adamw_rows(ddir, vectors, first, second, teacher)
    return (jnp.stack(grads), new_vectors, new_first, new_second, new_teacher)
```

```python
import jax
import jax.numpy as jnp
from jax import lax
from jax.sharding import Mesh, PartitionSpec as P

TILE = 16
AXES = ("z", "x", "crop", "y")


student_temp = 0.1
norm_eps = 1e-06
learn_rate = 0.01
weight_decay = 0.04
beta_first = 0.9
beta_second = 0.999
bias_first = 0.9999734386011124
bias_second = 0.0952078536
adam_eps = 1e-08
teacher_keep = 0.996


def swapped(shard):
    return lax.ppermute(shard, "crop", [(0, 1), (1, 0)])


def exchanged(blocks, axes):
    return lax.all_to_all(blocks, axes, 0, 0, tiled=True)


def copies(shard, axes):
    count = lax.axis_size(axes)
    return exchanged(jnp.broadcast_to(shard[None], (count,) + shard.shape), axes)


def norm_back(upstream, feats):
    length = jnp.sqrt(jnp.sum(feats * feats, 1, keepdims=True) + norm_eps)
    unit = feats / length
    return (upstream - unit * jnp.sum(unit * upstream, 1, keepdims=True)) / length


def adamw_rows(grad_rows, vectors, first, second, teacher):
    vlen = jnp.sqrt(jnp.sum(vectors * vectors, 1, keepdims=True) + norm_eps)
    unit = vectors / vlen
    dvec = (grad_rows - unit * jnp.sum(unit * grad_rows, 1, keepdims=True)) / vlen
    new_first = beta_first * first + (1.0 - beta_first) * dvec
    new_second = beta_second * second + (1.0 - beta_second) * dvec * dvec
    update = (
        new_first / bias_first / (jnp.sqrt(new_second / bias_second) + adam_eps)
        + weight_decay * vectors
    )
    new_vectors = vectors - learn_rate * update
    new_teacher = teacher_keep * teacher + (1.0 - teacher_keep) * new_vectors
    return (new_vectors, new_first, new_second, new_teacher)


def per_device(features, targets, partner, vectors, first, second, teacher):
    nz, nx, ny = lax.axis_size("z"), lax.axis_size("x"), lax.axis_size("y")
    own_rows, embed = features.shape[1:]
    crops = own_rows * nz * nx
    other = swapped(targets)
    feats = features[0].astype(jnp.float32)
    length = jnp.sqrt(jnp.sum(feats * feats, 1, keepdims=True) + norm_eps)
    unit_rows = (feats / length).astype(jnp.bfloat16)
    vlen = jnp.sqrt(jnp.sum(vectors * vectors, 1, keepdims=True) + norm_eps)
    own_direction = (vectors / vlen).astype(jnp.bfloat16)
    direction = lax.all_gather(own_direction, "crop", axis=0, tiled=True)
    unit_z = copies(unit_rows, "z").reshape(nz * own_rows, embed)
    unit_all = copies(unit_z, "x").reshape(crops, embed)
    leading = lax.axis_index("crop") == 0
    lower = jnp.where(leading, targets, other)
    upper = jnp.where(leading, other, targets)
    whole = jnp.concatenate([lower, upper], 0)
    ntiles = whole.shape[0] // TILE
    tiles = partner[0].reshape(nz, nx, own_rows // TILE).transpose(1, 0, 2).reshape(-1)
    picked = jnp.take(whole.reshape(ntiles, TILE, whole.shape[1]), tiles, axis=0)
    picked = picked.reshape(whole.shape[0], whole.shape[1]).astype(jnp.float32)
    scores = lax.dot_general(
        unit_all, direction, (((1,), (1,)), ((), ())), preferred_element_type=jnp.float32
    )
    expo = jnp.exp(scores / student_temp - 1.0 / student_temp)
    sums = jnp.stack([jnp.sum(expo, 1), jnp.sum(picked, 1)]).reshape(-1, 128)
    sums = jnp.sum(copies(sums, "z"), 0)
    sums = jnp.sum(copies(sums, ("x", "y")), 0).reshape(2, crops)
    exp_total, target_total = sums[0], sums[1]
    dscore = ((expo / exp_total[:, None] * target_total[:, None] - picked) / student_temp).astype(
        jnp.bfloat16
    )
    local_grad = lax.dot_general(
        dscore, unit_all, (((0,), (0,)), ((), ())), preferred_element_type=jnp.float32
    )
    owned = vectors.shape[0]
    core = lax.axis_index("crop")
    halves = local_grad.reshape(2, owned, embed)
    theirs = swapped(lax.dynamic_index_in_dim(halves, 1 - core, 0, keepdims=False))
    ddir = lax.dynamic_index_in_dim(halves, core, 0, keepdims=False) + theirs
    partial = jnp.dot(dscore, direction, preferred_element_type=jnp.float32)
    partial = partial.astype(jnp.bfloat16).reshape(nx, nz * own_rows, embed)
    partial = jnp.sum(exchanged(partial, "x").astype(jnp.float32), 0)
    partial = partial.astype(jnp.bfloat16).reshape(nz, own_rows, embed)
    partial = jnp.sum(exchanged(partial, "z").astype(jnp.float32), 0)
    dunit = jnp.sum(copies(partial, "y"), 0)
    grad_rows = norm_back(dunit, feats)
    new_vectors, new_first, new_second, new_teacher = adamw_rows(
        ddir, vectors, first, second, teacher
    )
    return (grad_rows[None], new_vectors, new_first, new_second, new_teacher)


def solution(mesh):
    shape = mesh.devices.shape
    apart = Mesh(mesh.devices.reshape(shape[0] // 4, 4, shape[1], shape[2]), AXES)
    rows = P(("z", "x", "y", "crop"), None)
    crops = P("crop", ("z", "x"), None)
    return jax.shard_map(
        per_device,
        mesh=apart,
        in_specs=(
            crops,
            P("crop", ("z", "x", "y")),
            P("crop", None),
            rows,
            rows,
            rows,
            rows,
        ),
        out_specs=(crops, rows, rows, rows, rows),
        check_vma=False,
    )
```

```python
import functools

import jax
import jax.numpy as jnp
from jax import lax
from jax.experimental import pallas as pl
from jax.experimental.pallas import tpu as pltpu
from jax.sharding import Mesh, PartitionSpec as P

TILE = 16
AXES = ("z", "x", "crop", "y")
PLANE = ("x", "y")
LANES = 128
BLOCK = 768


student_temp = 0.1
norm_eps = 1e-06
learn_rate = 0.01
weight_decay = 0.04
beta_first = 0.9
beta_second = 0.999
bias_first = 0.9999734386011124
bias_second = 0.0952078536
adam_eps = 1e-08
teacher_keep = 0.996


def swapped(shard):
    return lax.ppermute(shard, "crop", [(0, 1), (1, 0)])


def exchanged(blocks, axes):
    return lax.all_to_all(blocks, axes, 0, 0, tiled=True)


def norm_back(upstream, feats):
    length = jnp.sqrt(jnp.sum(feats * feats, 1, keepdims=True) + norm_eps)
    unit = feats / length
    return (upstream - unit * jnp.sum(unit * upstream, 1, keepdims=True)) / length


def adamw_rows(grad_rows, vectors, first, second, teacher):
    vlen = jnp.sqrt(jnp.sum(vectors * vectors, 1, keepdims=True) + norm_eps)
    unit = vectors / vlen
    dvec = (grad_rows - unit * jnp.sum(unit * grad_rows, 1, keepdims=True)) / vlen
    new_first = beta_first * first + (1.0 - beta_first) * dvec
    new_second = beta_second * second + (1.0 - beta_second) * dvec * dvec
    update = (
        new_first / bias_first / (jnp.sqrt(new_second / bias_second) + adam_eps)
        + weight_decay * vectors
    )
    new_vectors = vectors - learn_rate * update
    new_teacher = teacher_keep * teacher + (1.0 - teacher_keep) * new_vectors
    return (new_vectors, new_first, new_second, new_teacher)


def row_sums(block):
    folded = block[:, :LANES]
    for start in range(LANES, block.shape[1], LANES):
        folded = folded + block[:, start : start + LANES]
    return line_sums(folded)


def line_sums(folded):
    lines = []
    for start in range(0, folded.shape[0], LANES):
        lines.append(jnp.sum(folded[start : start + LANES].T, 0, keepdims=True))
    return jnp.concatenate(lines, 0)


def exponentials(unit, direction):
    scores = lax.dot_general(
        unit, direction, (((1,), (1,)), ((), ())), preferred_element_type=jnp.float32
    )
    return jnp.exp(scores * (1.0 / student_temp) - 1.0 / student_temp)


def picked_kernel(nz, partner_ref, core_ref, own_ref, other_ref, mine_ref, theirs_ref, picked_ref, sums_ref, direction_ref, whole, folded, halves, sems):
    slab = pl.program_id(0)
    nx = pl.num_programs(0)
    half = own_ref.shape[0]
    ny, rows, protos = picked_ref.shape
    few = TILE // ny
    per_dp = rows // few // nz

    @pl.when(slab == 0)
    def _():
        owned = mine_ref.shape[0]
        moves = [
            pltpu.make_async_copy(own_ref, whole.at[pl.ds(0, half)], sems.at[0]),
            pltpu.make_async_copy(other_ref, whole.at[pl.ds(half, half)], sems.at[1]),
            pltpu.make_async_copy(mine_ref, halves.at[0], sems.at[2]),
            pltpu.make_async_copy(theirs_ref, halves.at[1], sems.at[3]),
        ]
        for move in moves:
            move.start()
        for move in moves:
            move.wait()
        leading = core_ref[0] == 0
        mine = halves[0].astype(jnp.float32)
        theirs = halves[1].astype(jnp.float32)
        direction_ref[:owned, :] = jnp.where(leading, mine, theirs).astype(jnp.bfloat16)
        direction_ref[owned:, :] = jnp.where(leading, theirs, mine).astype(jnp.bfloat16)

    shift = core_ref[0] * half
    for group in range(rows // TILE):
        loaded = []
        for k in range(group * ny, (group + 1) * ny):
            z, tile = divmod(k, per_dp)
            wanted = partner_ref[z * nx * per_dp + slab * per_dp + tile] + shift
            wanted = jnp.where(wanted >= 2 * half, wanted - 2 * half, wanted)
            loaded.append(whole[wanted].astype(jnp.float32))
        place = slice(group * TILE, (group + 1) * TILE)
        for y in range(ny):
            piece = jnp.concatenate([tile[y * few : (y + 1) * few] for tile in loaded], 0)
            picked_ref[y, place, :] = piece.astype(jnp.bfloat16)
            total = piece[:, :LANES]
            for start in range(LANES, protos, LANES):
                total = total + piece[:, start : start + LANES]
            folded[y * rows + group * TILE : y * rows + (group + 1) * TILE, :] = total
    sums_ref[0] = line_sums(folded[...])


def picked_sums(partner, core, own, other, mine, theirs, nz, nx, ny):
    half, _, protos = own.shape
    owned, embed = mine.shape
    rows = 2 * half * TILE // (nx * ny)
    lines = ny * rows // LANES
    return pl.pallas_call(
        functools.partial(picked_kernel, nz),
        grid_spec=pltpu.PrefetchScalarGridSpec(
            num_scalar_prefetch=2,
            grid=(nx,),
            in_specs=[pl.BlockSpec(memory_space=pltpu.HBM)] * 4,
            out_specs=[
                pl.BlockSpec((ny, rows, protos), lambda i, p, c: (i, 0, 0)),
                pl.BlockSpec((1, lines, LANES), lambda i, p, c: (i, 0, 0)),
                pl.BlockSpec((2 * owned, embed), lambda i, p, c: (0, 0)),
            ],
            scratch_shapes=[
                pltpu.VMEM((2 * half, TILE, protos), jnp.bfloat16),
                pltpu.VMEM((ny * rows, LANES), jnp.float32),
                pltpu.VMEM((2, owned, embed), jnp.bfloat16),
                pltpu.SemaphoreType.DMA((4,)),
            ],
        ),
        out_shape=[
            jax.ShapeDtypeStruct((nx * ny, rows, protos), jnp.bfloat16),
            jax.ShapeDtypeStruct((nx, lines, LANES), jnp.float32),
            jax.ShapeDtypeStruct((2 * owned, embed), jnp.bfloat16),
        ],
        compiler_params=pltpu.CompilerParams(vmem_limit_bytes=60 << 20),
    )(partner, core, own, other, mine, theirs)


def halves_stacked(rows):
    return jnp.concatenate([rows[:, :LANES], rows[:, LANES:]], 0)


def halves_joined(stack):
    rows = stack.shape[0] // 2
    return jnp.concatenate([stack[:rows], stack[rows:]], 1)


def small_call(kernel, shape, dtype, *operands, scalars=0):
    specs = [pl.BlockSpec(memory_space=pltpu.SMEM)] * scalars
    specs += [pl.BlockSpec(memory_space=pltpu.VMEM)] * (len(operands) - scalars)
    return pl.pallas_call(
        kernel,
        in_specs=specs,
        out_specs=pl.BlockSpec(memory_space=pltpu.VMEM),
        out_shape=jax.ShapeDtypeStruct(shape, dtype),
        compiler_params=pltpu.CompilerParams(vmem_limit_bytes=8 << 20),
    )(*operands)


def unit_kernel(ny, y_ref, features_ref, out_ref):
    feats = features_ref[0].astype(jnp.float32)
    length = jnp.sqrt(jnp.sum(feats * feats, 1, keepdims=True) + norm_eps)
    unit = feats / length
    few = TILE // ny
    chosen = None
    for y in range(ny):
        rows = [unit[t + y * few : t + (y + 1) * few] for t in range(0, feats.shape[0], TILE)]
        rows = jnp.concatenate(rows, 0)
        chosen = rows if chosen is None else jnp.where(y_ref[0] == y, rows, chosen)
    stack = halves_stacked(chosen).astype(jnp.bfloat16)
    for z in range(out_ref.shape[0]):
        out_ref[z] = stack


def outgoing_kernel(unit_ref, out_ref):
    pieces = [halves_joined(unit_ref[z].astype(jnp.float32)) for z in range(unit_ref.shape[0])]
    own = jnp.concatenate(pieces, 0).astype(jnp.bfloat16)
    for chunk in range(out_ref.shape[0]):
        out_ref[chunk] = own


def plane_sum_kernel(in_ref, out_ref):
    total = in_ref[0].astype(jnp.float32)
    for chunk in range(1, in_ref.shape[0]):
        total = total + in_ref[chunk].astype(jnp.float32)
    count = out_ref.shape[0]
    part = total.shape[0] // count
    for z in range(count):
        out_ref[z] = halves_stacked(total[z * part : (z + 1) * part])


def grad_kernel(dunit_ref, features_ref, out_ref):
    ny, stack, _ = dunit_ref.shape
    few = TILE // ny
    parts = [halves_joined(dunit_ref[y]) for y in range(ny)]
    rows = []
    for t in range(0, stack // 2, few):
        rows += [parts[y][t : t + few] for y in range(ny)]
    out_ref[0] = norm_back(jnp.concatenate(rows, 0), features_ref[0].astype(jnp.float32))


def expo_kernel(unit_ref, direction_ref, sums_ref, out_ref, found):
    step = pl.program_id(0)
    expo = exponentials(unit_ref[...], direction_ref[...])
    found[step] = row_sums(expo)

    @pl.when(step == pl.num_programs(0) - 1)
    def _():
        parts = [found[k] for k in range(found.shape[0])]
        parts += [sums_ref[k] for k in range(sums_ref.shape[0])]
        message = jnp.concatenate(parts, 0).astype(jnp.bfloat16)
        for z in range(out_ref.shape[0]):
            out_ref[z] = message


def expo_sums(unit_all, direction, target_sums, nz):
    crops, embed = unit_all.shape
    protos = direction.shape[0]
    lines = 2 * crops // LANES
    return pl.pallas_call(
        expo_kernel,
        grid=(crops // BLOCK,),
        in_specs=[
            pl.BlockSpec((BLOCK, embed), lambda i: (i, 0)),
            pl.BlockSpec((protos, embed), lambda i: (0, 0)),
            pl.BlockSpec(target_sums.shape, lambda i: (0, 0, 0)),
        ],
        out_specs=pl.BlockSpec((nz, lines, LANES), lambda i: (0, 0, 0)),
        out_shape=jax.ShapeDtypeStruct((nz, lines, LANES), jnp.bfloat16),
        scratch_shapes=[pltpu.VMEM((crops // BLOCK, BLOCK // LANES, LANES), jnp.float32)],
        compiler_params=pltpu.CompilerParams(vmem_limit_bytes=16 << 20),
    )(unit_all, direction, target_sums)


def sum_copies_kernel(in_ref, out_ref):
    total = in_ref[0].astype(jnp.float32)
    for z in range(1, in_ref.shape[0]):
        total = total + in_ref[z].astype(jnp.float32)
    for chunk in range(out_ref.shape[0]):
        out_ref[chunk] = total


def dscore_kernel(core_ref, totals_ref, unit_ref, direction_ref, picked_ref, dunit_ref, keep_ref, send_ref, scale, dscore, ddir):
    step = pl.program_id(0)
    steps, lines, _ = scale.shape

    @pl.when(step == 0)
    def _():
        total = totals_ref[0]
        for chunk in range(1, totals_ref.shape[0]):
            total = total + totals_ref[chunk]
        factor = total[steps * lines :] / total[: steps * lines]
        for k in range(steps):
            scale[k] = factor[k * lines : (k + 1) * lines]

    expo = exponentials(unit_ref[...], direction_ref[...])
    factors = scale[step]
    for line in range(lines):
        rows = slice(line * LANES, (line + 1) * LANES)
        column = jnp.broadcast_to(factors[line : line + 1], (LANES, LANES)).T
        for start in range(0, dscore.shape[1], LANES):
            cols = slice(start, start + LANES)
            gap = expo[rows, cols] * column - picked_ref[rows, cols].astype(jnp.float32)
            dscore[rows, cols] = (gap * (1.0 / student_temp)).astype(jnp.bfloat16)
    dunit = jnp.dot(dscore[...], direction_ref[...], preferred_element_type=jnp.float32)
    dunit_ref[...] = dunit.astype(jnp.bfloat16)
    product = lax.dot_general(
        dscore[...], unit_ref[...], (((0,), (0,)), ((), ())), preferred_element_type=jnp.float32
    )

    @pl.when(step == 0)
    def _():
        ddir[...] = product

    @pl.when(step > 0)
    def _():
        ddir[...] += product

    @pl.when(step == steps - 1)
    def _():
        owned = keep_ref.shape[0]
        leading = core_ref[0] == 0
        keep_ref[...] = jnp.where(leading, ddir[:owned, :], ddir[owned:, :])
        send_ref[...] = jnp.where(leading, ddir[owned:, :], ddir[:owned, :])


def dunit_ddir(core, totals, unit_all, direction, picked):
    crops, embed = unit_all.shape
    protos = direction.shape[0]
    return pl.pallas_call(
        dscore_kernel,
        grid=(crops // BLOCK,),
        in_specs=[
            pl.BlockSpec(memory_space=pltpu.SMEM),
            pl.BlockSpec(totals.shape, lambda i: (0, 0, 0)),
            pl.BlockSpec((BLOCK, embed), lambda i: (i, 0)),
            pl.BlockSpec((protos, embed), lambda i: (0, 0)),
            pl.BlockSpec((BLOCK, protos), lambda i: (i, 0)),
        ],
        out_specs=[
            pl.BlockSpec((BLOCK, embed), lambda i: (i, 0)),
            pl.BlockSpec((protos // 2, embed), lambda i: (0, 0)),
            pl.BlockSpec((protos // 2, embed), lambda i: (0, 0)),
        ],
        out_shape=[
            jax.ShapeDtypeStruct((crops, embed), jnp.bfloat16),
            jax.ShapeDtypeStruct((protos // 2, embed), jnp.float32),
            jax.ShapeDtypeStruct((protos // 2, embed), jnp.float32),
        ],
        scratch_shapes=[
            pltpu.VMEM((crops // BLOCK, BLOCK // LANES, LANES), jnp.float32),
            pltpu.VMEM((BLOCK, protos), jnp.bfloat16),
            pltpu.VMEM((protos, embed), jnp.float32),
        ],
        compiler_params=pltpu.CompilerParams(vmem_limit_bytes=16 << 20),
    )(core, totals, unit_all, direction, picked)


def per_device(features, targets, partner, vectors, first, second, teacher):
    nz, nx, ny = lax.axis_size("z"), lax.axis_size("x"), lax.axis_size("y")
    core = lax.axis_index("crop")[None].astype(jnp.int32)
    y_index = lax.axis_index("y")[None].astype(jnp.int32)
    own_rows, embed = features.shape[1:]
    part = own_rows // ny
    stack = 2 * part
    crops = nz * nx * own_rows
    chunks = nx * ny
    half, protos = targets.shape
    other = swapped(targets)
    unit_z = small_call(
        functools.partial(unit_kernel, ny),
        (nz, stack, LANES),
        jnp.bfloat16,
        y_index,
        features,
        scalars=1,
    )
    unit_z = exchanged(unit_z, "z")
    vlen = jnp.sqrt(jnp.sum(vectors * vectors, 1, keepdims=True) + norm_eps)
    own_direction = (vectors / vlen).astype(jnp.bfloat16)
    other_direction = swapped(own_direction)
    picked, target_sums, direction = picked_sums(
        partner[0],
        core,
        targets.reshape(half // TILE, TILE, protos),
        other.reshape(half // TILE, TILE, protos),
        own_direction,
        other_direction,
        nz,
        nx,
        ny,
    )
    unit_z, target_sums, picked, direction = lax.optimization_barrier(
        (unit_z, target_sums, picked, direction)
    )
    unit_all = small_call(outgoing_kernel, (chunks, nz * part, embed), jnp.bfloat16, unit_z)
    unit_all = exchanged(unit_all, PLANE).reshape(crops, embed)
    sums = exchanged(expo_sums(unit_all, direction, target_sums, nz), "z")
    totals = small_call(sum_copies_kernel, (chunks,) + sums.shape[1:], jnp.float32, sums)
    totals = exchanged(totals, PLANE)
    picked = picked.reshape(crops, protos)
    partial, ours, sent = dunit_ddir(core, totals, unit_all, direction, picked)
    theirs = swapped(sent)
    partial = exchanged(partial.reshape(chunks, nz * part, embed), PLANE)
    partial = small_call(plane_sum_kernel, (nz, stack, LANES), jnp.float32, partial)
    partial = exchanged(partial, "z")
    partial, theirs, ours = lax.optimization_barrier((partial, theirs, ours))
    partial = small_call(sum_copies_kernel, (ny, stack, LANES), jnp.float32, partial)
    dunit = exchanged(partial, "y")
    grad_rows = small_call(grad_kernel, features.shape, jnp.float32, dunit, features)
    new_vectors, new_first, new_second, new_teacher = adamw_rows(
        ours + theirs, vectors, first, second, teacher
    )
    return (grad_rows, new_vectors, new_first, new_second, new_teacher)


def solution(mesh):
    shape = mesh.devices.shape
    apart = Mesh(mesh.devices.reshape(shape[0] // 4, 4, shape[1], shape[2]), AXES)
    rows = P(("z", "x", "y", "crop"), None)
    crops = P("crop", ("z", "x"), None)
    return jax.shard_map(
        per_device,
        mesh=apart,
        in_specs=(
            crops,
            P("crop", ("z", "x", "y")),
            P("crop", None),
            rows,
            rows,
            rows,
            rows,
        ),
        out_specs=(crops, rows, rows, rows, rows),
        check_vma=False,
    )
```

```python
import functools

import jax
import jax.numpy as jnp
from jax import lax
from jax.experimental import pallas as pl
from jax.experimental.pallas import tpu as pltpu
from jax.sharding import Mesh, PartitionSpec as P

TILE = 16
AXES = ("z", "x", "crop", "y")
PLANE = ("x", "y")
LANES = 128
BLOCK = 768


student_temp = 0.1
norm_eps = 1e-06
learn_rate = 0.01
weight_decay = 0.04
beta_first = 0.9
beta_second = 0.999
bias_first = 0.9999734386011124
bias_second = 0.0952078536
adam_eps = 1e-08
teacher_keep = 0.996


def swapped(shard):
    return lax.ppermute(shard, "crop", [(0, 1), (1, 0)])


def exchanged(blocks, axes):
    return lax.all_to_all(blocks, axes, 0, 0, tiled=True)


def norm_back(upstream, feats):
    length = jnp.sqrt(jnp.sum(feats * feats, 1, keepdims=True) + norm_eps)
    unit = feats / length
    return (upstream - unit * jnp.sum(unit * upstream, 1, keepdims=True)) / length


def adamw_rows(grad_rows, vectors, first, second, teacher):
    vlen = jnp.sqrt(jnp.sum(vectors * vectors, 1, keepdims=True) + norm_eps)
    unit = vectors / vlen
    dvec = (grad_rows - unit * jnp.sum(unit * grad_rows, 1, keepdims=True)) / vlen
    new_first = beta_first * first + (1.0 - beta_first) * dvec
    new_second = beta_second * second + (1.0 - beta_second) * dvec * dvec
    update = (
        new_first / bias_first / (jnp.sqrt(new_second / bias_second) + adam_eps)
        + weight_decay * vectors
    )
    new_vectors = vectors - learn_rate * update
    new_teacher = teacher_keep * teacher + (1.0 - teacher_keep) * new_vectors
    return (new_vectors, new_first, new_second, new_teacher)


def row_sums(block):
    folded = block[:, :LANES]
    for start in range(LANES, block.shape[1], LANES):
        folded = folded + block[:, start : start + LANES]
    return line_sums(folded)


def line_sums(folded):
    lines = []
    for start in range(0, folded.shape[0], LANES):
        lines.append(jnp.sum(folded[start : start + LANES].T, 0, keepdims=True))
    return jnp.concatenate(lines, 0)


def exponentials(unit, direction):
    scores = lax.dot_general(
        unit, direction, (((1,), (1,)), ((), ())), preferred_element_type=jnp.float32
    )
    return jnp.exp(scores * (1.0 / student_temp) - 1.0 / student_temp)


def picked_kernel(nz, partner_ref, core_ref, own_ref, other_ref, picked_ref, sums_ref, whole, folded, sems):
    slab = pl.program_id(0)
    nx = pl.num_programs(0)
    half = own_ref.shape[0]
    ny, rows, protos = picked_ref.shape
    few = TILE // ny
    per_dp = rows // few // nz

    @pl.when(slab == 0)
    def _():
        moves = [
            pltpu.make_async_copy(own_ref, whole.at[pl.ds(0, half)], sems.at[0]),
            pltpu.make_async_copy(other_ref, whole.at[pl.ds(half, half)], sems.at[1]),
        ]
        for move in moves:
            move.start()
        for move in moves:
            move.wait()

    shift = core_ref[0] * half
    for group in range(rows // TILE):
        loaded = []
        for k in range(group * ny, (group + 1) * ny):
            z, tile = divmod(k, per_dp)
            wanted = partner_ref[z * nx * per_dp + slab * per_dp + tile] + shift
            wanted = jnp.where(wanted >= 2 * half, wanted - 2 * half, wanted)
            loaded.append(whole[wanted].astype(jnp.float32))
        place = slice(group * TILE, (group + 1) * TILE)
        for y in range(ny):
            piece = jnp.concatenate([tile[y * few : (y + 1) * few] for tile in loaded], 0)
            picked_ref[y, place, :] = piece.astype(jnp.bfloat16)
            total = piece[:, :LANES]
            for start in range(LANES, protos, LANES):
                total = total + piece[:, start : start + LANES]
            folded[y * rows + group * TILE : y * rows + (group + 1) * TILE, :] = total
    sums_ref[0] = line_sums(folded[...])


def picked_sums(partner, core, own, other, nz, nx, ny):
    half, _, protos = own.shape
    rows = 2 * half * TILE // (nx * ny)
    lines = ny * rows // LANES
    return pl.pallas_call(
        functools.partial(picked_kernel, nz),
        grid_spec=pltpu.PrefetchScalarGridSpec(
            num_scalar_prefetch=2,
            grid=(nx,),
            in_specs=[pl.BlockSpec(memory_space=pltpu.HBM)] * 2,
            out_specs=[
                pl.BlockSpec((ny, rows, protos), lambda i, p, c: (i, 0, 0)),
                pl.BlockSpec((1, lines, LANES), lambda i, p, c: (i, 0, 0)),
            ],
            scratch_shapes=[
                pltpu.VMEM((2 * half, TILE, protos), jnp.bfloat16),
                pltpu.VMEM((ny * rows, LANES), jnp.float32),
                pltpu.SemaphoreType.DMA((2,)),
            ],
        ),
        out_shape=[
            jax.ShapeDtypeStruct((nx * ny, rows, protos), jnp.bfloat16),
            jax.ShapeDtypeStruct((nx, lines, LANES), jnp.float32),
        ],
        compiler_params=pltpu.CompilerParams(vmem_limit_bytes=60 << 20),
    )(partner, core, own, other)


def halves_stacked(rows):
    return jnp.concatenate([rows[:, :LANES], rows[:, LANES:]], 0)


def halves_joined(stack):
    rows = stack.shape[0] // 2
    return jnp.concatenate([stack[:rows], stack[rows:]], 1)


def plain_call(kernel, outs, *operands, scalars=0, scratch=(), limit=8):
    specs = [pl.BlockSpec(memory_space=pltpu.SMEM)] * scalars
    specs += [pl.BlockSpec(memory_space=pltpu.VMEM)] * (len(operands) - scalars)
    return pl.pallas_call(
        kernel,
        in_specs=specs,
        out_specs=[pl.BlockSpec(memory_space=pltpu.VMEM)] * len(outs),
        out_shape=[jax.ShapeDtypeStruct(*out) for out in outs],
        scratch_shapes=list(scratch),
        compiler_params=pltpu.CompilerParams(vmem_limit_bytes=limit << 20),
    )(*operands)


def small_call(kernel, shape, dtype, *operands, scalars=0):
    return plain_call(kernel, [(shape, dtype)], *operands, scalars=scalars)[0]


def direction_kernel(vectors_ref, out_ref):
    vectors = vectors_ref[...]
    vlen = jnp.sqrt(jnp.sum(vectors * vectors, 1, keepdims=True) + norm_eps)
    out_ref[...] = (vectors / vlen).astype(jnp.bfloat16)


def unit_kernel(ny, y_ref, features_ref, out_ref):
    feats = features_ref[0].astype(jnp.float32)
    length = jnp.sqrt(jnp.sum(feats * feats, 1, keepdims=True) + norm_eps)
    unit = feats / length
    few = TILE // ny
    chosen = None
    for y in range(ny):
        rows = [unit[t + y * few : t + (y + 1) * few] for t in range(0, feats.shape[0], TILE)]
        rows = jnp.concatenate(rows, 0)
        chosen = rows if chosen is None else jnp.where(y_ref[0] == y, rows, chosen)
    stack = halves_stacked(chosen).astype(jnp.bfloat16)
    for z in range(out_ref.shape[0]):
        out_ref[z] = stack


def outgoing_kernel(unit_ref, out_ref):
    pieces = [halves_joined(unit_ref[z].astype(jnp.float32)) for z in range(unit_ref.shape[0])]
    own = jnp.concatenate(pieces, 0).astype(jnp.bfloat16)
    for chunk in range(out_ref.shape[0]):
        out_ref[chunk] = own


def plane_sum_kernel(in_ref, out_ref):
    total = in_ref[0].astype(jnp.float32)
    for chunk in range(1, in_ref.shape[0]):
        total = total + in_ref[chunk].astype(jnp.float32)
    count = out_ref.shape[0]
    part = total.shape[0] // count
    for z in range(count):
        out_ref[z] = halves_stacked(total[z * part : (z + 1) * part])


def grad_kernel(dunit_ref, features_ref, out_ref):
    ny, stack, _ = dunit_ref.shape
    few = TILE // ny
    parts = [halves_joined(dunit_ref[y]) for y in range(ny)]
    rows = []
    for t in range(0, stack // 2, few):
        rows += [parts[y][t : t + few] for y in range(ny)]
    out_ref[0] = norm_back(jnp.concatenate(rows, 0), features_ref[0].astype(jnp.float32))


def expo_kernel(core_ref, unit_ref, mine_ref, theirs_ref, sums_ref, out_ref, direction_ref, expo_ref, found):
    owned = mine_ref.shape[0]
    leading = core_ref[0] == 0
    mine = mine_ref[...].astype(jnp.float32)
    theirs = theirs_ref[...].astype(jnp.float32)
    direction_ref[:owned, :] = jnp.where(leading, mine, theirs).astype(jnp.bfloat16)
    direction_ref[owned:, :] = jnp.where(leading, theirs, mine).astype(jnp.bfloat16)

    def block(step, carry):
        rows = pl.ds(pl.multiple_of(step * BLOCK, BLOCK), BLOCK)
        expo = exponentials(unit_ref[rows, :], direction_ref[...])
        expo_ref[rows, :] = expo
        found[step] = row_sums(expo)
        return carry

    lax.fori_loop(0, found.shape[0], block, 0)
    parts = [found[k] for k in range(found.shape[0])]
    parts += [sums_ref[k] for k in range(sums_ref.shape[0])]
    message = jnp.concatenate(parts, 0).astype(jnp.bfloat16)
    for z in range(out_ref.shape[0]):
        out_ref[z] = message


def expo_sums(core, unit_all, mine, theirs, target_sums, nz):
    crops, embed = unit_all.shape
    return plain_call(
        expo_kernel,
        [
            ((nz, 2 * crops // LANES, LANES), jnp.bfloat16),
            ((2 * mine.shape[0], embed), jnp.bfloat16),
            ((crops, 2 * mine.shape[0]), jnp.float32),
        ],
        core,
        unit_all,
        mine,
        theirs,
        target_sums,
        scalars=1,
        scratch=[pltpu.VMEM((crops // BLOCK, BLOCK // LANES, LANES), jnp.float32)],
        limit=16,
    )


def sum_copies_kernel(in_ref, out_ref):
    total = in_ref[0].astype(jnp.float32)
    for z in range(1, in_ref.shape[0]):
        total = total + in_ref[z].astype(jnp.float32)
    for chunk in range(out_ref.shape[0]):
        out_ref[chunk] = total.astype(out_ref.dtype)


def dscore_kernel(totals_ref, expo_ref, direction_ref, picked_ref, dunit_ref, dscore_ref, scale):
    steps, lines, _ = scale.shape
    total = totals_ref[0].astype(jnp.float32)
    for chunk in range(1, totals_ref.shape[0]):
        total = total + totals_ref[chunk].astype(jnp.float32)
    factor = total[steps * lines :] / total[: steps * lines]
    for k in range(steps):
        scale[k] = factor[k * lines : (k + 1) * lines]

    def block(step, carry):
        first = pl.multiple_of(step * BLOCK, BLOCK)
        own = pl.ds(first, BLOCK)
        factors = scale[step]
        for line in range(lines):
            rows = pl.ds(pl.multiple_of(first + line * LANES, LANES), LANES)
            column = jnp.broadcast_to(factors[line : line + 1], (LANES, LANES)).T
            for start in range(0, dscore_ref.shape[1], LANES):
                cols = slice(start, start + LANES)
                gap = expo_ref[rows, cols] * column - picked_ref[rows, cols].astype(jnp.float32)
                dscore_ref[rows, cols] = (gap * (1.0 / student_temp)).astype(jnp.bfloat16)
        dunit = jnp.dot(dscore_ref[own, :], direction_ref[...], preferred_element_type=jnp.float32)
        dunit_ref[own, :] = dunit.astype(jnp.bfloat16)
        return carry

    lax.fori_loop(0, steps, block, 0)


def dscore_dunit(totals, expo, direction, picked):
    crops, protos = expo.shape
    return plain_call(
        dscore_kernel,
        [((crops, direction.shape[1]), jnp.bfloat16), ((crops, protos), jnp.bfloat16)],
        totals,
        expo,
        direction,
        picked,
        scratch=[pltpu.VMEM((crops // BLOCK, BLOCK // LANES, LANES), jnp.float32)],
        limit=24,
    )


def ddir_kernel(core_ref, dscore_ref, unit_ref, keep_ref, send_ref):
    ddir = jnp.zeros((dscore_ref.shape[1], unit_ref.shape[1]), jnp.float32)
    for first in range(0, dscore_ref.shape[0], BLOCK):
        ddir = ddir + lax.dot_general(
            dscore_ref[first : first + BLOCK, :],
            unit_ref[first : first + BLOCK, :],
            (((0,), (0,)), ((), ())),
            preferred_element_type=jnp.float32,
        )
    owned = keep_ref.shape[0]
    leading = core_ref[0] == 0
    keep_ref[...] = jnp.where(leading, ddir[:owned], ddir[owned:])
    send_ref[...] = jnp.where(leading, ddir[owned:], ddir[:owned])


def per_device(features, targets, partner, vectors, first, second, teacher):
    nz, nx, ny = lax.axis_size("z"), lax.axis_size("x"), lax.axis_size("y")
    core = lax.axis_index("crop")[None].astype(jnp.int32)
    y_index = lax.axis_index("y")[None].astype(jnp.int32)
    own_rows, embed = features.shape[1:]
    part = own_rows // ny
    stack = 2 * part
    crops = nz * nx * own_rows
    chunks = nx * ny
    half, protos = targets.shape
    other = swapped(targets)
    unit_z = small_call(
        functools.partial(unit_kernel, ny),
        (nz, stack, LANES),
        jnp.bfloat16,
        y_index,
        features,
        scalars=1,
    )
    unit_z = exchanged(unit_z, "z")
    unit_z, vectors, own_targets = lax.optimization_barrier((unit_z, vectors, targets))
    own_direction = small_call(direction_kernel, vectors.shape, jnp.bfloat16, vectors)
    other_direction = swapped(own_direction)
    picked, target_sums = picked_sums(
        partner[0],
        core,
        own_targets.reshape(half // TILE, TILE, protos),
        other.reshape(half // TILE, TILE, protos),
        nz,
        nx,
        ny,
    )
    unit_all = small_call(outgoing_kernel, (chunks, nz * part, embed), jnp.bfloat16, unit_z)
    unit_all = exchanged(unit_all, PLANE).reshape(crops, embed)
    sums, direction, expo = expo_sums(core, unit_all, own_direction, other_direction, target_sums, nz)
    sums = exchanged(sums, "z")
    totals = small_call(sum_copies_kernel, (chunks,) + sums.shape[1:], jnp.bfloat16, sums)
    totals = exchanged(totals, PLANE)
    picked = picked.reshape(crops, protos)
    partial, dscore = dscore_dunit(totals, expo, direction, picked)
    partial = exchanged(partial.reshape(chunks, nz * part, embed), PLANE)
    partial, dscore = lax.optimization_barrier((partial, dscore))
    half_rows = (vectors.shape, jnp.float32)
    ours, sent = plain_call(
        ddir_kernel, [half_rows, half_rows], core, dscore, unit_all, scalars=1, limit=16
    )
    theirs = swapped(sent)
    partial = small_call(plane_sum_kernel, (nz, stack, LANES), jnp.float32, partial)
    partial = exchanged(partial, "z")
    partial, theirs, ours = lax.optimization_barrier((partial, theirs, ours))
    partial = small_call(sum_copies_kernel, (ny, stack, LANES), jnp.float32, partial)
    dunit = exchanged(partial, "y")
    grad_rows = small_call(grad_kernel, features.shape, jnp.float32, dunit, features)
    new_vectors, new_first, new_second, new_teacher = adamw_rows(
        ours + theirs, vectors, first, second, teacher
    )
    return (grad_rows, new_vectors, new_first, new_second, new_teacher)


def solution(mesh):
    shape = mesh.devices.shape
    apart = Mesh(mesh.devices.reshape(shape[0] // 4, 4, shape[1], shape[2]), AXES)
    rows = P(("z", "x", "y", "crop"), None)
    crops = P("crop", ("z", "x"), None)
    return jax.shard_map(
        per_device,
        mesh=apart,
        in_specs=(
            crops,
            P("crop", ("z", "x", "y")),
            P("crop", None),
            rows,
            rows,
            rows,
            rows,
        ),
        out_specs=(crops, rows, rows, rows, rows),
        check_vma=False,
    )
```

```python
import functools

import jax
import jax.numpy as jnp
from jax import lax
from jax.experimental import pallas as pl
from jax.experimental.pallas import tpu as pltpu
from jax.sharding import Mesh, PartitionSpec as P

TILE = 16
AXES = ("z", "x", "crop", "y")
PLANE = ("x", "y")
LANES = 128
BLOCK = 768


student_temp = 0.1
norm_eps = 1e-06
learn_rate = 0.01
weight_decay = 0.04
beta_first = 0.9
beta_second = 0.999
bias_first = 0.9999734386011124
bias_second = 0.0952078536
adam_eps = 1e-08
teacher_keep = 0.996


def swapped(shard):
    return lax.ppermute(shard, "crop", [(0, 1), (1, 0)])


def exchanged(blocks, axes):
    return lax.all_to_all(blocks, axes, 0, 0, tiled=True)


def norm_back(upstream, feats):
    length = jnp.sqrt(jnp.sum(feats * feats, 1, keepdims=True) + norm_eps)
    unit = feats / length
    return (upstream - unit * jnp.sum(unit * upstream, 1, keepdims=True)) / length


def adamw_rows(grad_rows, vectors, first, second, teacher):
    vlen = jnp.sqrt(jnp.sum(vectors * vectors, 1, keepdims=True) + norm_eps)
    unit = vectors / vlen
    dvec = (grad_rows - unit * jnp.sum(unit * grad_rows, 1, keepdims=True)) / vlen
    new_first = beta_first * first + (1.0 - beta_first) * dvec
    new_second = beta_second * second + (1.0 - beta_second) * dvec * dvec
    update = (
        new_first / bias_first / (jnp.sqrt(new_second / bias_second) + adam_eps)
        + weight_decay * vectors
    )
    new_vectors = vectors - learn_rate * update
    new_teacher = teacher_keep * teacher + (1.0 - teacher_keep) * new_vectors
    return (new_vectors, new_first, new_second, new_teacher)


def row_sums(block):
    folded = block[:, :LANES]
    for start in range(LANES, block.shape[1], LANES):
        folded = folded + block[:, start : start + LANES]
    return line_sums(folded)


def line_sums(folded):
    lines = []
    for start in range(0, folded.shape[0], LANES):
        lines.append(jnp.sum(folded[start : start + LANES].T, 0, keepdims=True))
    return jnp.concatenate(lines, 0)


def exponentials(unit, direction):
    scores = lax.dot_general(
        unit, direction, (((1,), (1,)), ((), ())), preferred_element_type=jnp.float32
    )
    return jnp.exp(scores * (1.0 / student_temp) - 1.0 / student_temp)


def picked_kernel(nz, partner_ref, core_ref, own_ref, other_ref, picked_ref, sums_ref, whole, folded, sems):
    slab = pl.program_id(0)
    nx = pl.num_programs(0)
    half = own_ref.shape[0]
    ny, rows, protos = picked_ref.shape
    few = TILE // ny
    per_dp = rows // few // nz

    @pl.when(slab == 0)
    def _():
        moves = [
            pltpu.make_async_copy(own_ref, whole.at[pl.ds(0, half)], sems.at[0]),
            pltpu.make_async_copy(other_ref, whole.at[pl.ds(half, half)], sems.at[1]),
        ]
        for move in moves:
            move.start()
        for move in moves:
            move.wait()

    shift = core_ref[0] * half
    for group in range(rows // TILE):
        loaded = []
        for k in range(group * ny, (group + 1) * ny):
            z, tile = divmod(k, per_dp)
            wanted = partner_ref[z * nx * per_dp + slab * per_dp + tile] + shift
            wanted = jnp.where(wanted >= 2 * half, wanted - 2 * half, wanted)
            loaded.append(whole[wanted].astype(jnp.float32))
        place = slice(group * TILE, (group + 1) * TILE)
        for y in range(ny):
            piece = jnp.concatenate([tile[y * few : (y + 1) * few] for tile in loaded], 0)
            picked_ref[y, place, :] = piece.astype(jnp.bfloat16)
            total = piece[:, :LANES]
            for start in range(LANES, protos, LANES):
                total = total + piece[:, start : start + LANES]
            folded[y * rows + group * TILE : y * rows + (group + 1) * TILE, :] = total
    sums_ref[0] = line_sums(folded[...])


def picked_sums(partner, core, own, other, nz, nx, ny):
    half, _, protos = own.shape
    rows = 2 * half * TILE // (nx * ny)
    lines = ny * rows // LANES
    return pl.pallas_call(
        functools.partial(picked_kernel, nz),
        grid_spec=pltpu.PrefetchScalarGridSpec(
            num_scalar_prefetch=2,
            grid=(nx,),
            in_specs=[pl.BlockSpec(memory_space=pltpu.HBM)] * 2,
            out_specs=[
                pl.BlockSpec((ny, rows, protos), lambda i, p, c: (i, 0, 0)),
                pl.BlockSpec((1, lines, LANES), lambda i, p, c: (i, 0, 0)),
            ],
            scratch_shapes=[
                pltpu.VMEM((2 * half, TILE, protos), jnp.bfloat16),
                pltpu.VMEM((ny * rows, LANES), jnp.float32),
                pltpu.SemaphoreType.DMA((2,)),
            ],
        ),
        out_shape=[
            jax.ShapeDtypeStruct((nx * ny, rows, protos), jnp.bfloat16),
            jax.ShapeDtypeStruct((nx, lines, LANES), jnp.float32),
        ],
        compiler_params=pltpu.CompilerParams(vmem_limit_bytes=60 << 20),
    )(partner, core, own, other)


def halves_stacked(rows):
    return jnp.concatenate([rows[:, :LANES], rows[:, LANES:]], 0)


def halves_joined(stack):
    rows = stack.shape[0] // 2
    return jnp.concatenate([stack[:rows], stack[rows:]], 1)


def plain_call(kernel, outs, *operands, scalars=0, scratch=(), limit=8):
    specs = [pl.BlockSpec(memory_space=pltpu.SMEM)] * scalars
    specs += [pl.BlockSpec(memory_space=pltpu.VMEM)] * (len(operands) - scalars)
    return pl.pallas_call(
        kernel,
        in_specs=specs,
        out_specs=[pl.BlockSpec(memory_space=pltpu.VMEM)] * len(outs),
        out_shape=[jax.ShapeDtypeStruct(*out) for out in outs],
        scratch_shapes=list(scratch),
        compiler_params=pltpu.CompilerParams(vmem_limit_bytes=limit << 20),
    )(*operands)


def small_call(kernel, shape, dtype, *operands, scalars=0):
    return plain_call(kernel, [(shape, dtype)], *operands, scalars=scalars)[0]


def direction_kernel(vectors_ref, out_ref):
    vectors = vectors_ref[...]
    vlen = jnp.sqrt(jnp.sum(vectors * vectors, 1, keepdims=True) + norm_eps)
    out_ref[...] = (vectors / vlen).astype(jnp.bfloat16)


def unit_kernel(ny, y_ref, features_ref, out_ref):
    feats = features_ref[0].astype(jnp.float32)
    length = jnp.sqrt(jnp.sum(feats * feats, 1, keepdims=True) + norm_eps)
    unit = feats / length
    few = TILE // ny
    chosen = None
    for y in range(ny):
        rows = [unit[t + y * few : t + (y + 1) * few] for t in range(0, feats.shape[0], TILE)]
        rows = jnp.concatenate(rows, 0)
        chosen = rows if chosen is None else jnp.where(y_ref[0] == y, rows, chosen)
    stack = halves_stacked(chosen).astype(jnp.bfloat16)
    for z in range(out_ref.shape[0]):
        out_ref[z] = stack


def outgoing_kernel(unit_ref, out_ref):
    pieces = [halves_joined(unit_ref[z].astype(jnp.float32)) for z in range(unit_ref.shape[0])]
    own = jnp.concatenate(pieces, 0).astype(jnp.bfloat16)
    for chunk in range(out_ref.shape[0]):
        out_ref[chunk] = own


def plane_sum_kernel(in_ref, out_ref):
    total = in_ref[0].astype(jnp.float32)
    for chunk in range(1, in_ref.shape[0]):
        total = total + in_ref[chunk].astype(jnp.float32)
    count = out_ref.shape[0]
    part = total.shape[0] // count
    for z in range(count):
        out_ref[z] = halves_stacked(total[z * part : (z + 1) * part])


def grad_kernel(dunit_ref, features_ref, out_ref):
    ny, stack, _ = dunit_ref.shape
    few = TILE // ny
    parts = [halves_joined(dunit_ref[y]) for y in range(ny)]
    rows = []
    for t in range(0, stack // 2, few):
        rows += [parts[y][t : t + few] for y in range(ny)]
    out_ref[0] = norm_back(jnp.concatenate(rows, 0), features_ref[0].astype(jnp.float32))


def expo_kernel(core_ref, unit_ref, mine_ref, theirs_ref, sums_ref, out_ref, direction_ref, expo_ref, found):
    owned = mine_ref.shape[0]
    leading = core_ref[0] == 0
    mine = mine_ref[...].astype(jnp.float32)
    theirs = theirs_ref[...].astype(jnp.float32)
    direction_ref[:owned, :] = jnp.where(leading, mine, theirs).astype(jnp.bfloat16)
    direction_ref[owned:, :] = jnp.where(leading, theirs, mine).astype(jnp.bfloat16)

    def block(step, carry):
        rows = pl.ds(pl.multiple_of(step * BLOCK, BLOCK), BLOCK)
        expo = exponentials(unit_ref[rows, :], direction_ref[...])
        expo_ref[rows, :] = expo
        found[step] = row_sums(expo)
        return carry

    lax.fori_loop(0, found.shape[0], block, 0)
    parts = [found[k] for k in range(found.shape[0])]
    parts += [sums_ref[k] for k in range(sums_ref.shape[0])]
    message = jnp.concatenate(parts, 0).astype(jnp.bfloat16)
    for z in range(out_ref.shape[0]):
        out_ref[z] = message


def expo_sums(core, unit_all, mine, theirs, target_sums, nz):
    crops, embed = unit_all.shape
    return plain_call(
        expo_kernel,
        [
            ((nz, 2 * crops // LANES, LANES), jnp.bfloat16),
            ((2 * mine.shape[0], embed), jnp.bfloat16),
            ((crops, 2 * mine.shape[0]), jnp.float32),
        ],
        core,
        unit_all,
        mine,
        theirs,
        target_sums,
        scalars=1,
        scratch=[pltpu.VMEM((crops // BLOCK, BLOCK // LANES, LANES), jnp.float32)],
        limit=16,
    )


def sum_copies_kernel(in_ref, out_ref):
    total = in_ref[0].astype(jnp.float32)
    for z in range(1, in_ref.shape[0]):
        total = total + in_ref[z].astype(jnp.float32)
    for chunk in range(out_ref.shape[0]):
        out_ref[chunk] = total.astype(out_ref.dtype)


def dscore_kernel(totals_ref, expo_ref, direction_ref, picked_ref, dunit_ref, dscore_ref, scale):
    steps, lines, _ = scale.shape
    total = totals_ref[0].astype(jnp.float32)
    for chunk in range(1, totals_ref.shape[0]):
        total = total + totals_ref[chunk].astype(jnp.float32)
    factor = total[steps * lines :] / total[: steps * lines]
    for k in range(steps):
        scale[k] = factor[k * lines : (k + 1) * lines]

    def block(step, carry):
        first = pl.multiple_of(step * BLOCK, BLOCK)
        own = pl.ds(first, BLOCK)
        factors = scale[step]
        for line in range(lines):
            rows = pl.ds(pl.multiple_of(first + line * LANES, LANES), LANES)
            column = jnp.broadcast_to(factors[line : line + 1], (LANES, LANES)).T
            for start in range(0, dscore_ref.shape[1], LANES):
                cols = slice(start, start + LANES)
                gap = expo_ref[rows, cols] * column - picked_ref[rows, cols].astype(jnp.float32)
                dscore_ref[rows, cols] = (gap * (1.0 / student_temp)).astype(jnp.bfloat16)
        dunit = jnp.dot(dscore_ref[own, :], direction_ref[...], preferred_element_type=jnp.float32)
        dunit_ref[own, :] = dunit.astype(jnp.bfloat16)
        return carry

    lax.fori_loop(0, steps, block, 0)


def dscore_dunit(totals, expo, direction, picked):
    crops, protos = expo.shape
    return plain_call(
        dscore_kernel,
        [((crops, direction.shape[1]), jnp.bfloat16), ((crops, protos), jnp.bfloat16)],
        totals,
        expo,
        direction,
        picked,
        scratch=[pltpu.VMEM((crops // BLOCK, BLOCK // LANES, LANES), jnp.float32)],
        limit=24,
    )


def ddir_kernel(core_ref, dscore_ref, unit_ref, keep_ref, send_ref):
    ddir = jnp.zeros((dscore_ref.shape[1], unit_ref.shape[1]), jnp.float32)
    for first in range(0, dscore_ref.shape[0], BLOCK):
        ddir = ddir + lax.dot_general(
            dscore_ref[first : first + BLOCK, :],
            unit_ref[first : first + BLOCK, :],
            (((0,), (0,)), ((), ())),
            preferred_element_type=jnp.float32,
        )
    owned = keep_ref.shape[0]
    leading = core_ref[0] == 0
    keep_ref[...] = jnp.where(leading, ddir[:owned], ddir[owned:])
    send_ref[...] = jnp.where(leading, ddir[owned:], ddir[:owned])


def per_device(features, targets, partner, vectors, first, second, teacher):
    nz, nx, ny = lax.axis_size("z"), lax.axis_size("x"), lax.axis_size("y")
    core = lax.axis_index("crop")[None].astype(jnp.int32)
    y_index = lax.axis_index("y")[None].astype(jnp.int32)
    own_rows, embed = features.shape[1:]
    part = own_rows // ny
    stack = 2 * part
    crops = nz * nx * own_rows
    chunks = nx * ny
    half, protos = targets.shape
    other = swapped(targets)
    unit_z = small_call(
        functools.partial(unit_kernel, ny),
        (nz, stack, LANES),
        jnp.bfloat16,
        y_index,
        features,
        scalars=1,
    )
    unit_z = exchanged(unit_z, "z")
    unit_z, own_targets = lax.optimization_barrier((unit_z, targets))
    own_direction = small_call(direction_kernel, vectors.shape, jnp.bfloat16, vectors)
    other_direction = swapped(own_direction)
    picked, target_sums = picked_sums(
        partner[0],
        core,
        own_targets.reshape(half // TILE, TILE, protos),
        other.reshape(half // TILE, TILE, protos),
        nz,
        nx,
        ny,
    )
    unit_all = small_call(outgoing_kernel, (chunks, nz * part, embed), jnp.bfloat16, unit_z)
    unit_all = exchanged(unit_all, PLANE).reshape(crops, embed)
    sums, direction, expo = expo_sums(core, unit_all, own_direction, other_direction, target_sums, nz)
    sums = exchanged(sums, "z")
    totals = small_call(sum_copies_kernel, (chunks,) + sums.shape[1:], jnp.bfloat16, sums)
    totals = exchanged(totals, PLANE)
    picked = picked.reshape(crops, protos)
    partial, dscore = dscore_dunit(totals, expo, direction, picked)
    partial = exchanged(partial.reshape(chunks, nz * part, embed), PLANE)
    partial, dscore = lax.optimization_barrier((partial, dscore))
    half_rows = (vectors.shape, jnp.float32)
    ours, sent = plain_call(
        ddir_kernel, [half_rows, half_rows], core, dscore, unit_all, scalars=1, limit=16
    )
    theirs = swapped(sent)
    partial = small_call(plane_sum_kernel, (nz, stack, LANES), jnp.float32, partial)
    partial = exchanged(partial, "z")
    partial, theirs, ours = lax.optimization_barrier((partial, theirs, ours))
    partial = small_call(sum_copies_kernel, (ny, stack, LANES), jnp.float32, partial)
    dunit = exchanged(partial, "y")
    grad_rows = small_call(grad_kernel, features.shape, jnp.float32, dunit, features)
    new_vectors, new_first, new_second, new_teacher = adamw_rows(
        ours + theirs, vectors, first, second, teacher
    )
    return (grad_rows, new_vectors, new_first, new_second, new_teacher)


def solution(mesh):
    shape = mesh.devices.shape
    apart = Mesh(mesh.devices.reshape(shape[0] // 4, 4, shape[1], shape[2]), AXES)
    rows = P(("z", "x", "y", "crop"), None)
    crops = P("crop", ("z", "x"), None)
    return jax.shard_map(
        per_device,
        mesh=apart,
        in_specs=(
            crops,
            P("crop", ("z", "x", "y")),
            P("crop", None),
            rows,
            rows,
            rows,
            rows,
        ),
        out_specs=(crops, rows, rows, rows, rows),
        check_vma=False,
    )
```
